1024 devices in a mesh: region: 128 (over z, y), local: 8 (over x, core).
Axes of the slice: x: 4, y: 4, z: 32, core: 2. Of those that a mesh axis runs over, the one named last changes fastest.
Arguments:
- atm_flux: bfloat16 [12, 4194304], P(None, ('region', 'local')), may hold values from -6 to 6
- cell_map: int32 [1024, 4096], P(('region', 'local')), may hold values from 0 to 4095, each once within a row
- neighbours: int32 [4, 4194304], P(None, ('region', 'local')), may hold values from 0 to 4095
- coef_x: float32 [4, 4194304], P(None, ('region', 'local')), may hold values from -3 to 3
- coef_y: float32 [4, 4194304], P(None, ('region', 'local')), may hold values from -3 to 3
- send_list: int32 [1024, 8, 4], P(('region', 'local')), may hold values from 0 to 31, as said below
- cover: int32 [4096, 4], P(('region', 'local')), may hold values from 0 to 31, as said below
- cover_count: int32 [4096], P(('region', 'local')), may hold values from 1 to 4
- weights: bfloat16 [4096, 4, 3, 128, 128], P(('region', 'local')), may hold values from -0.15625 to 0.15625
- ocean_map: int32 [1024, 512], P(('region', 'local')), may hold values from 0 to 511, each once within a row
Outputs:
- ocean_flux: float32 [12, 524288], P(None, ('region', 'local'))
The draws below stay inside these ranges and needn't reach their ends.
Inputs may be any that keep to these rules, and one draw needn't show every extreme that they name: `cell_map`: each row is a permutation of one device's cells. `neighbours`: indices of coupler cells on the same device. `send_list`: each row lists 4 different source blocks of the sending device. `cover`: each row lists 4 different slots of what the owner receives from its region. `ocean_map`: each row is a permutation of one device's ocean cells.
All inputs are finite; a program needn't handle non-finite values.
Results may differ from the reference program's by a relative error of at most 0.0024.
Values may be sent and summed in bfloat16 or wider, within the bound.
A program may use at most 64 MiB of HBM per device.

```python
import jax
import jax.numpy as jnp
from jax import lax

F = 12
BS = 128
OS = 128
NB = 4
K = 4
CAP = 4
A_DEV = 4096
OBLK = 4
NDEV = 1024
ABLK = 32
O_DEV = 512
ACELLS = 4194304
OBLOCKS = 4096
N_REGION = 128
N_LOCAL = 8


def draw_send_list(key, part):
    key = jax.random.fold_in(key, 11)
    base = jnp.broadcast_to(jnp.arange(ABLK, dtype=jnp.int32), (NDEV, N_LOCAL, ABLK))
    shuffled = jax.random.permutation(key, base, axis=2, independent=True)
    return shuffled[:, :, :CAP].astype(jnp.int32)


def draw_cover(key, part):
    key = jax.random.fold_in(key, 23)
    base = jnp.broadcast_to(jnp.arange(N_LOCAL * CAP, dtype=jnp.int32), (OBLOCKS, N_LOCAL * CAP))
    shuffled = jax.random.permutation(key, base, axis=1, independent=True)
    return shuffled[:, :K].astype(jnp.int32)


def place_ends(array, stream_key, least, largest):
    index_at = [jax.random.randint(jax.random.fold_in(stream_key, axis), (), 0, length) for axis, length in enumerate(array.shape)]
    widest = array.shape.index(max(array.shape))
    beside = index_at[:widest] + [(index_at[widest] + 1) % array.shape[widest]] + index_at[widest + 1:]
    return array.at[tuple(index_at)].set(least).at[tuple(beside)].set(largest)


def shard_levels(stream_key, shape, shards, least, top_value):
    loudness, own = 1.0, jax.random.fold_in(stream_key, 6)
    for axis_at, shards_of in shards:
        steps = jnp.exp(jax.random.uniform(jax.random.fold_in(own, axis_at), (shards_of,), jnp.float32, least / len(shards), top_value / len(shards)))
        loudness = loudness * jnp.repeat(steps, shape[axis_at] // shards_of).reshape([-1 if axis == axis_at else 1 for axis in range(len(shape))])
    return loudness


def centred(own_key, shape, deviation, most, pieces=(), kind=jnp.bfloat16):
    values = jax.random.normal(own_key, shape, jnp.float32) * deviation
    if len(pieces) > 0:
        values = shard_levels(own_key, shape, pieces, -0.22, 0.18) * values
    return jnp.clip(values, min=-most, max=most).astype(kind)


def setup_inputs(seed: int = 0) -> dict:
    key_of = jax.random.split(jax.random.key(seed), 11)
    return {
        "atm_flux": centred(key_of[0], (F, ACELLS), 1.0, 6.0, ((1, 1024),)),
        "cell_map": jax.vmap(lambda own: jax.random.permutation(own, A_DEV))(jax.random.split(key_of[1], NDEV)).reshape((NDEV, A_DEV)).astype(jnp.int32),
        "neighbours": place_ends(jax.random.randint(key_of[2], (NB, ACELLS), 0, A_DEV), jax.random.fold_in(key_of[2], 1), 0, A_DEV - 1).astype(jnp.int32),
        "coef_x": centred(key_of[3], (NB, ACELLS), 0.5, 3.0, ((1, 1024),), jnp.float32),
        "coef_y": centred(key_of[4], (NB, ACELLS), 0.5, 3.0, ((1, 1024),), jnp.float32),
        "send_list": draw_send_list(jax.random.fold_in(key_of[10], 71), 0),
        "cover": draw_cover(jax.random.fold_in(key_of[10], 71), 0),
        "cover_count": place_ends(jax.random.randint(key_of[7], (OBLOCKS,), 1, K + 1), jax.random.fold_in(key_of[7], 1), 1, K).astype(jnp.int32),
        "weights": centred(key_of[8], (OBLOCKS, K, 3, OS, BS), (3 * K * BS) ** -0.5, 0.15625, ((0, 1024),)),
        "ocean_map": jax.vmap(lambda own: jax.random.permutation(own, O_DEV))(jax.random.split(key_of[9], NDEV)).reshape((NDEV, O_DEV)).astype(jnp.int32),
    }


def reconstruct(values, near_index, weight_x, weight_y):
    nearby = values[:, near_index]
    change = nearby - values[:, None, :]
    slope_x = jnp.sum(weight_x[None] * change, axis=1)
    slope_y = jnp.sum(weight_y[None] * change, axis=1)
    upper = jnp.maximum(values, jnp.max(nearby, axis=1))
    lower = jnp.minimum(values, jnp.min(nearby, axis=1))
    steep = jnp.abs(slope_x) + jnp.abs(slope_y)
    factor = jnp.minimum(1.0, (upper - lower) / jnp.maximum(steep, 1.0))
    return jnp.stack([values, factor * slope_x, factor * slope_y]).astype(jnp.bfloat16)


def reconstruct_packed(packed):
    return reconstruct(packed[0], packed[1], packed[2], packed[3])


def reference(atm_flux, cell_map, neighbours, coef_x, coef_y, send_list, cover, cover_count, weights, ocean_map):
    devices = N_REGION * N_LOCAL
    piece = A_DEV // devices
    source = atm_flux.reshape(F, devices, A_DEV)
    ordered = jnp.take_along_axis(source, cell_map[None], axis=2)
    coupled = ordered.reshape(F, devices, devices, piece).transpose(2, 0, 1, 3)
    coupled = coupled.reshape(devices, F, A_DEV).astype(jnp.float32)
    near_dev = neighbours.reshape(NB, devices, A_DEV).transpose(1, 0, 2)
    along_x = coef_x.reshape(NB, devices, A_DEV).transpose(1, 0, 2)
    along_y = coef_y.reshape(NB, devices, A_DEV).transpose(1, 0, 2)
    recon = lax.map(reconstruct_packed, (coupled, near_dev, along_x, along_y))
    recon = recon.reshape(devices, 3, F, A_DEV // BS, BS)
    cover_dev = cover.reshape(devices, OBLK, K)
    count_dev = cover_count.reshape(devices, OBLK)
    weight_dev = weights.reshape(devices, OBLK, K, 3, OS, BS)

    def remap_one(packed):
        device, covers, counts, block_weights = packed
        region = device // N_LOCAL
        member = device % N_LOCAL
        sender = region * N_LOCAL + covers // CAP
        blocks = send_list[sender, member, covers % CAP]
        chosen = recon[sender, :, :, blocks]
        live = (jnp.arange(K, dtype=jnp.int32)[None, :] < counts[:, None]).astype(jnp.float32)
        chosen = chosen.astype(jnp.float32) * live[:, :, None, None, None]
        result = jnp.einsum("bkmos,bkmfs->fbo", block_weights.astype(jnp.float32), chosen,
                            precision=lax.Precision.HIGHEST)
        return result.reshape(F, OBLK * OS)

    remapped = lax.map(remap_one, (jnp.arange(devices, dtype=jnp.int32), cover_dev, count_dev, weight_dev))
    leaving = jnp.take_along_axis(remapped, ocean_map[:, None, :], axis=2)
    share = O_DEV // N_REGION
    ocean = leaving.reshape(N_REGION, N_LOCAL, F, N_REGION, share).transpose(2, 3, 1, 0, 4)
    return ocean.reshape(F, devices * O_DEV)
```

```python
import jax
import jax.numpy as jnp
from jax import lax
from jax.experimental import pallas as pl
from jax.experimental.pallas import tpu as pltpu
from jax.sharding import PartitionSpec as P

MESH = pl.DeviceIdType.MESH
F = 12
FP = 16
Z, Y, L = 32, 4, 8
YL = Y * L
NB = 4
K = 4
CAP = 4
OBLK = 4
BS = 128
ABLK = 32
ROWS = 3 * FP
FAR_FIRST = sorted(range(1, Z), key=lambda i: -min(i, Z - i))


def pick(table, index):
    return jnp.take_along_axis(table, index, axis=1, mode="promise_in_bounds")


def spread(row):
    return jnp.broadcast_to(row, (8, BS))


def swap_blocks(parts, turned):
    lane = lax.broadcasted_iota(jnp.int32, (32, BS), 1)
    turned[...] = jnp.concatenate(parts, axis=0).T
    rows = [turned[pl.ds(g, 32, stride=4), :] for g in range(4)]
    result = []
    for i in range(len(parts)):
        index = i * 32 + (lane >> 2)
        total = pick(rows[0], index)
        for g in range(1, 4):
            total = jnp.where((lane & 3) == g, pick(rows[g], index), total)
        result.append(total)
    return result


def swap_fields(source, target, turned):
    for q in range(F // 4):
        parts = [source[pl.ds(4 * q + i, 32, stride=FP), :] for i in range(4)]
        for i, part in enumerate(swap_blocks(parts, turned.at[q])):
            target[pl.ds(4 * q + i, 32, stride=FP), :] = part


def look_up(table, ranks, rows):
    columns = []
    for row in rows:
        low = jnp.broadcast_to((row & 255).astype(jnp.float32), (16, BS)).astype(jnp.bfloat16)
        low = jnp.broadcast_to(low[None], (16, 16, BS)).reshape(256, BS)
        one, zero = jnp.ones((256, BS), jnp.bfloat16), jnp.zeros((256, BS), jnp.bfloat16)
        columns.append(jnp.where(ranks[...] == low, one, zero))
    product = jnp.dot(table[...], jnp.concatenate(columns, axis=1), preferred_element_type=jnp.float32)
    found = []
    for i, row in enumerate(rows):
        high = jnp.broadcast_to(row >> 8, (FP, BS))
        lanes = slice(i * BS, (i + 1) * BS)
        value = product[:FP, lanes]
        for h in range(1, 16):
            value = jnp.where(high == h, product[h * FP : (h + 1) * FP, lanes], value)
        found.append(value)
    return found


def kernel(
    atm_hbm,
    cell_map_hbm,
    neighbours_hbm,
    coef_x_hbm,
    coef_y_hbm,
    send_list_hbm,
    cover_hbm,
    cover_count_hbm,
    weights_hbm,
    ocean_map_hbm,
    out,
    atm,
    cell_map,
    neighbours,
    coef_x,
    coef_y,
    send_list,
    cover,
    cover_count,
    weights,
    ocean_map,
    ranks,
    pairs,
    table,
    mixed,
    turned,
    map_rows,
    recon,
    remapped,
    landed,
    turned_out,
    send_a,
    recv_a,
    send_b,
    recv_b,
    send_c,
    recv_c,
    send_d,
    recv_e,
    loaded,
    sent,
    arrived,
):
    region, member = lax.axis_index("region"), lax.axis_index("local")
    z, y = region // Y, region % Y
    yl = y * L + member

    def plane_peer(i):
        other = (yl + i) % YL
        return other, {"region": z * Y + other // L, "local": other % L}

    def column_peer(i):
        other = (z + i) % Z
        return other, {"region": other * Y + y, "local": member}

    def send(source, target, phase, device):
        pltpu.make_async_remote_copy(
            src_ref=source,
            dst_ref=target,
            send_sem=sent.at[phase],
            recv_sem=arrived.at[phase],
            device_id=device,
            device_id_type=MESH,
        ).start()

    def wait(buffer, semaphore):
        pltpu.make_async_copy(buffer, buffer, semaphore).wait()

    loads = [
        pltpu.make_async_copy(source, target, loaded.at[i])
        for i, (source, target) in enumerate(
            (
                (cell_map_hbm, cell_map),
                (atm_hbm, atm),
                (neighbours_hbm, neighbours),
                (coef_x_hbm, coef_x),
                (coef_y_hbm, coef_y),
                (send_list_hbm, send_list),
                (cover_hbm, cover),
                (cover_count_hbm, cover_count),
                (ocean_map_hbm, ocean_map),
                (weights_hbm, weights),
            )
        )
    ]
    barrier = pltpu.get_barrier_semaphore()

    for i in FAR_FIRST:
        pl.semaphore_signal(barrier, inc=1, device_id=column_peer(i)[1], device_id_type=MESH)

    @pl.loop(1, YL)
    def _(i):
        pl.semaphore_signal(barrier, inc=1, device_id=plane_peer(i)[1], device_id_type=MESH)

    for load in loads:
        load.start()

    ranks[...] = lax.broadcasted_iota(jnp.int32, (256, BS), 0).astype(jnp.float32).astype(jnp.bfloat16)
    for load in loads[:2]:
        load.wait()
    for h in range(32):
        lanes = slice(h * BS, (h + 1) * BS)
        start, parity = (h // 2) * FP, h % 2
        pairs[pl.ds(start, F), parity * BS : (parity + 1) * BS] = atm[:, lanes]
        map_rows[pl.ds(h, 1), :] = cell_map[:, lanes]
    cells = map_rows[...].astype(jnp.float32)
    map_rows[...] = swap_blocks([cells] * 4, turned.at[0])[0].astype(jnp.int32)

    @pl.loop(0, YL // 8)
    def _(n):
        for half in range(2):
            rows = [map_rows[pl.ds(n * 8 + half * 4 + i, 1), :] for i in range(4)]
            for i, found in enumerate(look_up(pairs, ranks, rows)):
                send_a[n * 8 + half * 4 + i] = found[:F].astype(jnp.bfloat16)

    pl.semaphore_wait(barrier, 2 * 31)

    @pl.loop(1, YL)
    def _(i):
        other, device = plane_peer(i)
        send(send_a.at[other], recv_a.at[yl], 0, device)

    recv_a[yl] = send_a[yl]
    for load in loads[2:]:
        load.wait()
    wait(recv_a.at[pl.ds(0, YL - 1)], arrived.at[0])

    for a in range(YL):
        mixed[pl.ds(a * FP, F), :] = recv_a[a].astype(jnp.float32)
    swap_fields(mixed, table, turned)
    for c in range(Z):
        send_b[c] = table[pl.ds(c * FP, F), :].astype(jnp.bfloat16)

    for i in FAR_FIRST:
        other, device = column_peer(i)
        send(send_b.at[other], recv_b.at[z], 1, device)

    recv_b[z] = send_b[z]
    wait(recv_b.at[pl.ds(0, Z - 1)], arrived.at[1])
    for h in range(32):
        parity = h % 2
        pairs[pl.ds((h // 2) * FP, F), parity * BS : (parity + 1) * BS] = recv_b[h]

    def reconstruct(b):
        lanes = pl.ds(pl.multiple_of(b * BS, BS), BS)
        near, along_x, along_y = neighbours[:, lanes], coef_x[:, lanes], coef_y[:, lanes]
        value = recv_b[b].astype(jnp.float32)
        nearby = [found[:F] for found in look_up(pairs, ranks, [near[j : j + 1] for j in range(NB)])]
        change = [found - value for found in nearby]
        slope_x = sum(along_x[j : j + 1] * change[j] for j in range(NB))
        slope_y = sum(along_y[j : j + 1] * change[j] for j in range(NB))
        upper, lower = value, value
        for found in nearby:
            upper, lower = jnp.maximum(upper, found), jnp.minimum(lower, found)
        steep = jnp.abs(slope_x) + jnp.abs(slope_y)
        factor = jnp.minimum(1.0, (upper - lower) / jnp.maximum(steep, 1.0))
        for m, term in enumerate((value, factor * slope_x, factor * slope_y)):
            recon[b, m * FP : m * FP + F, :] = term.astype(jnp.bfloat16)

    @pl.loop(0, 8)
    def _(n):
        for i in range(4):
            reconstruct(n * 4 + i)

    def gather_blocks(other):
        for k in range(CAP):
            send_c[other, k] = recon[send_list[0, k, other]]

    @pl.loop(1, L)
    def _(i):
        other = (member + i) % L
        gather_blocks(other)
        send(send_c.at[other], recv_c.at[pl.ds(member * CAP, CAP)], 2, {"region": region, "local": other})

    gather_blocks(member)
    for k in range(CAP):
        recv_c[member * CAP + k] = send_c[member, k]
    wait(recv_c.at[pl.ds(0, (L - 1) * CAP)], arrived.at[2])

    for o in range(OBLK):
        total = jnp.zeros((FP, BS), jnp.float32)
        for k in range(K):
            chosen = recv_c[cover[o, k]]
            part = jnp.zeros((FP, BS), jnp.float32)
            for m in range(3):
                part += lax.dot_general(
                    chosen[m * FP : (m + 1) * FP],
                    weights[(o * K + k) * 3 + m],
                    (((1,), (1,)), ((), ())),
                    preferred_element_type=jnp.float32,
                )
            live = jnp.minimum(jnp.maximum(cover_count[o] - k, 0), 1).astype(jnp.float32)
            total += part * live
        remapped[pl.ds(o * FP, FP), :] = total

    lane = lax.broadcasted_iota(jnp.int32, (8, BS), 1)
    row = lax.broadcasted_iota(jnp.int32, (8, BS), 0)
    for q in range(4):
        cells = pick(spread(ocean_map[:, q * BS : (q + 1) * BS]), row * 16 + (lane & 15))
        block, within = cells >> 7, cells & 127
        for a in range(2):
            total = jnp.zeros((8, BS), jnp.float32)
            for b in range(min(8, F - 8 * a)):
                value = jnp.zeros((8, BS), jnp.float32)
                for o in range(OBLK):
                    near = pick(spread(remapped[pl.ds(o * FP + 8 * a + b, 1), :]), within)
                    value = jnp.where(block == o, near, value)
                total = jnp.where((lane >> 4) == b, value, total)
            for s in range(8):
                send_d[q * 8 + s, :, a * BS : (a + 1) * BS] = total[s : s + 1, :]

    for i in FAR_FIRST:
        other, device = column_peer(i)
        send(send_d.at[other], recv_e.at[y, z], 3, device)

    recv_e[y, z] = send_d[z]
    wait(send_d.at[pl.ds(0, Z - 1)], arrived.at[3])

    @pl.loop(1, Y)
    def _(i):
        other = (y + i) % Y
        send(recv_e.at[y], recv_e.at[y], 4, {"region": z * Y + other, "local": member})

    wait(recv_e.at[pl.ds(0, Y - 1)], arrived.at[4])
    for s in range(Y):
        for t in range(Z):
            landed[pl.ds(s * Z + t, 1), :] = recv_e[s, t]
    for a in range(2):
        turned_out[a] = landed[:, a * BS : (a + 1) * BS].T
        rows = [turned_out[a, pl.ds(y * 4 + p, 8, stride=16), :] for p in range(4)]
        height = min(8, F - 8 * a)
        for c in range(4):
            index = ((lane >> 2) & 3) * 32 + c * 8 + (lane >> 4)
            total = pick(rows[0], index)
            for p in range(1, 4):
                total = jnp.where((lane & 3) == p, pick(rows[p], index), total)
            out[pl.ds(a * 8, height), c * BS : (c + 1) * BS] = total[:height]

    wait(send_a.at[pl.ds(0, YL - 1)], sent.at[0])
    wait(send_b.at[pl.ds(0, Z - 1)], sent.at[1])
    wait(send_c.at[pl.ds(0, L - 1)], sent.at[2])
    wait(send_d.at[pl.ds(0, Z - 1)], sent.at[3])
    wait(recv_e.at[pl.ds(0, Y - 1)], sent.at[4])


def shards(
    atm_flux,
    cell_map,
    neighbours,
    coef_x,
    coef_y,
    send_list,
    cover,
    cover_count,
    weights,
    ocean_map,
):
    vmem = pl.BlockSpec(memory_space=pltpu.VMEM)
    blocks = weights.reshape(OBLK * K * 3, BS, BS)
    f32, bf16 = jnp.float32, jnp.bfloat16
    return pl.pallas_call(
        kernel,
        out_shape=jax.ShapeDtypeStruct((F, OBLK * BS), f32),
        in_specs=[pl.BlockSpec(memory_space=pltpu.HBM)] * 10,
        out_specs=vmem,
        scratch_shapes=[
            pltpu.VMEM(atm_flux.shape, bf16),
            pltpu.VMEM(cell_map.shape, jnp.int32),
            pltpu.VMEM(neighbours.shape, jnp.int32),
            pltpu.VMEM(coef_x.shape, f32),
            pltpu.VMEM(coef_y.shape, f32),
            pltpu.SMEM((1, CAP, L), jnp.int32),
            pltpu.SMEM(cover.shape, jnp.int32),
            pltpu.SMEM(cover_count.shape, jnp.int32),
            pltpu.VMEM(blocks.shape, bf16),
            pltpu.VMEM(ocean_map.shape, jnp.int32),
            pltpu.VMEM((256, BS), bf16),
            pltpu.VMEM((16 * FP, 2 * BS), bf16),
            pltpu.VMEM((32 * FP, BS), f32),
            pltpu.VMEM((32 * FP, BS), f32),
            pltpu.VMEM((F // 4, BS, BS), f32),
            pltpu.VMEM((32, BS), jnp.int32),
            pltpu.VMEM((ABLK, ROWS, BS), bf16),
            pltpu.VMEM((OBLK * FP, BS), f32),
            pltpu.VMEM((Y * Z, 2 * BS), f32),
            pltpu.VMEM((2, BS, BS), f32),
            pltpu.VMEM((YL, F, BS), bf16),
            pltpu.VMEM((YL, F, BS), bf16),
            pltpu.VMEM((Z, F, BS), bf16),
            pltpu.VMEM((Z, F, BS), bf16),
            pltpu.VMEM((L, CAP, ROWS, BS), bf16),
            pltpu.VMEM((L * CAP, ROWS, BS), bf16),
            pltpu.VMEM((Z, 1, 2 * BS), f32),
            pltpu.VMEM((Y, Z, 1, 2 * BS), f32),
            pltpu.SemaphoreType.DMA((10,)),
            pltpu.SemaphoreType.DMA((5,)),
            pltpu.SemaphoreType.DMA((5,)),
        ],
        compiler_params=pltpu.CompilerParams(
            collective_id=0, has_side_effects=True, vmem_limit_bytes=62 * 2**20
        ),
    )(
        atm_flux,
        cell_map,
        neighbours,
        coef_x,
        coef_y,
        jnp.swapaxes(send_list, 1, 2),
        cover,
        cover_count,
        blocks,
        ocean_map,
    )


def solution(mesh):
    return jax.shard_map(
        shards,
        mesh=mesh,
        in_specs=(
            P(None, ("region", "local")),
            P(("region", "local"), None),
            P(None, ("region", "local")),
            P(None, ("region", "local")),
            P(None, ("region", "local")),
            P(("region", "local"), None, None),
            P(("region", "local"), None),
            P(("region", "local")),
            P(("region", "local"), None, None, None, None),
            P(("region", "local"), None),
        ),
        out_specs=P(None, ("region", "local")),
        check_vma=False,
    )
```

```python
import jax
import jax.numpy as jnp
from jax import lax
from jax.experimental import pallas as pl
from jax.experimental.pallas import tpu as pltpu
from jax.sharding import PartitionSpec as P

MESH = pl.DeviceIdType.MESH
F = 12
FP = 16
Z, Y, L = 32, 4, 8
YL = Y * L
NB = 4
K = 4
CAP = 4
OBLK = 4
BS = 128
ABLK = 32
FAR_FIRST = sorted(range(1, Z), key=lambda i: -min(i, Z - i))


def pick(table, index):
    return jnp.take_along_axis(table, index, axis=1, mode="promise_in_bounds")


def spread(row):
    return jnp.broadcast_to(row, (8, BS))


def swap_blocks(parts, turned):
    lane = lax.broadcasted_iota(jnp.int32, (32, BS), 1)
    turned[...] = jnp.concatenate(parts, axis=0).T
    rows = [turned[pl.ds(g, 32, stride=4), :] for g in range(4)]
    result = []
    for i in range(len(parts)):
        index = i * 32 + (lane >> 2)
        total = pick(rows[0], index)
        for g in range(1, 4):
            total = jnp.where((lane & 3) == g, pick(rows[g], index), total)
        result.append(total)
    return result


def swap_fields(source, target, turned):
    for q in range(F // 4):
        parts = [source[pl.ds(4 * q + i, 32, stride=FP), :] for i in range(4)]
        for i, part in enumerate(swap_blocks(parts, turned.at[q])):
            target[pl.ds(4 * q + i, 32, stride=FP), :] = part


def one_hot(ranks, rows):
    columns = []
    for row in rows:
        low = jnp.broadcast_to((row & 255).astype(jnp.float32), (16, BS)).astype(jnp.bfloat16)
        low = jnp.broadcast_to(low[None], (16, 16, BS)).reshape(256, BS)
        one, zero = jnp.ones((256, BS), jnp.bfloat16), jnp.zeros((256, BS), jnp.bfloat16)
        columns.append(jnp.where(ranks[...] == low, one, zero))
    return jnp.concatenate(columns, axis=1)


def fill_pairs(pairs, table):
    for parity in range(2):
        lanes = slice(parity * BS, (parity + 1) * BS)
        starts = [(2 * h + parity) * FP for h in range(16)]
        for p in range(8):
            rows = [table[pl.ds(start, 8), :] for start in starts[2 * p : 2 * p + 2]]
            pairs[pl.ds(16 * p, 16), lanes] = jnp.concatenate(rows, axis=0).astype(jnp.bfloat16)
        for p in range(4):
            rows = [table[pl.ds(start + 8, 4), :] for start in starts[4 * p : 4 * p + 4]]
            pairs[pl.ds(128 + 16 * p, 16), lanes] = jnp.concatenate(rows, axis=0).astype(jnp.bfloat16)


def high_part(row):
    return jnp.broadcast_to(row >> 8, (8, BS))


def select_eight(product, high):
    value = product[:8]
    for h in range(1, 16):
        value = jnp.where(high == h, product[8 * h : 8 * h + 8], value)
    return value


def select_four(product, high):
    own = high - (lax.broadcasted_iota(jnp.int32, (8, BS), 0) >> 2)
    value = jnp.zeros((8, BS), jnp.float32)
    for p in range(8):
        value = jnp.where(own == 2 * p, product[8 * p : 8 * p + 8], value)
    return value[:4] + value[4:]


def multiply(table, columns):
    return jnp.dot(table, columns, preferred_element_type=jnp.float32)


def gradients(value, nearby, along_x, along_y):
    change = [found - value for found in nearby]
    slope_x = sum(along_x[j : j + 1] * change[j] for j in range(NB))
    slope_y = sum(along_y[j : j + 1] * change[j] for j in range(NB))
    upper, lower = value, value
    for found in nearby:
        upper, lower = jnp.maximum(upper, found), jnp.minimum(lower, found)
    steep = jnp.abs(slope_x) + jnp.abs(slope_y)
    factor = jnp.minimum(1.0, (upper - lower) / jnp.maximum(steep, 1.0))
    return value, factor * slope_x, factor * slope_y


def kernel(
    atm_hbm,
    cell_map_hbm,
    neighbours_hbm,
    coef_x_hbm,
    coef_y_hbm,
    send_list_hbm,
    cover_hbm,
    cover_count_hbm,
    weights_hbm,
    ocean_map_hbm,
    out,
    atm,
    cell_map,
    neighbours,
    coef_x,
    coef_y,
    send_list,
    cover,
    cover_count,
    weights,
    ocean_map,
    ranks,
    columns,
    pairs,
    table,
    mixed,
    turned,
    map_rows,
    recon_8,
    recon_4,
    remapped,
    landed,
    turned_out,
    send_a,
    recv_a,
    send_b,
    recv_b,
    send_c,
    recv_c,
    send_f,
    recv_f,
    send_d,
    recv_e,
    loaded,
    sent,
    arrived,
    reach,
):
    region, member = lax.axis_index("region"), lax.axis_index("local")
    z, y = region // Y, region % Y
    yl = y * L + member

    def plane_peer(i):
        other = (yl + i) % YL
        return other, {"region": z * Y + other // L, "local": other % L}

    def column_peer(i):
        other = (z + i) % Z
        return other, {"region": other * Y + y, "local": member}

    def send(source, target, phase, device):
        pltpu.make_async_remote_copy(
            src_ref=source,
            dst_ref=target,
            send_sem=sent.at[phase],
            recv_sem=arrived.at[phase],
            device_id=device,
            device_id_type=MESH,
        ).start()

    def wait(buffer, semaphore):
        pltpu.make_async_copy(buffer, buffer, semaphore).wait()

    loads = [
        pltpu.make_async_copy(source, target, loaded.at[i])
        for i, (source, target) in enumerate(
            (
                (cell_map_hbm, cell_map),
                (atm_hbm, atm),
                (neighbours_hbm, neighbours),
                (coef_x_hbm, coef_x),
                (coef_y_hbm, coef_y),
                (send_list_hbm, send_list),
                (cover_hbm, cover),
                (cover_count_hbm, cover_count),
                (ocean_map_hbm, ocean_map),
                (weights_hbm, weights),
            )
        )
    ]
    barrier = pltpu.get_barrier_semaphore()

    for i in (1, Z - 1):
        pl.semaphore_signal(barrier, inc=1, device_id=column_peer(i)[1], device_id_type=MESH)

    @pl.loop(1, YL)
    def _(i):
        pl.semaphore_signal(barrier, inc=1, device_id=plane_peer(i)[1], device_id_type=MESH)

    def tell(step):
        for i in (2**step, Z - 2**step):
            pl.semaphore_signal(
                reach.at[step], inc=1, device_id=column_peer(i)[1], device_id_type=MESH
            )

    def hear(step):
        pl.semaphore_wait(reach.at[step], 2)

    for load in loads:
        load.start()

    pl.semaphore_wait(barrier, YL - 1 + 2)
    tell(0)
    hear(0)
    tell(1)

    ranks[...] = lax.broadcasted_iota(jnp.int32, (256, BS), 0).astype(jnp.float32).astype(jnp.bfloat16)
    for load in loads[:2]:
        load.wait()
    for h in range(32):
        lanes = slice(h * BS, (h + 1) * BS)
        table[pl.ds(h * FP, F), :] = atm[:, lanes].astype(jnp.float32)
        map_rows[pl.ds(h, 1), :] = cell_map[:, lanes]
    fill_pairs(pairs, table)
    cells = map_rows[...].astype(jnp.float32)
    map_rows[...] = swap_blocks([cells] * 4, turned.at[0])[0].astype(jnp.int32)

    @pl.loop(0, YL // 8)
    def _(n):
        for half in range(2):
            rows = [map_rows[pl.ds(n * 8 + half * 4 + i, 1), :] for i in range(4)]
            product = multiply(pairs[...], one_hot(ranks, rows))
            for i, row in enumerate(rows):
                part, high = product[:, i * BS : (i + 1) * BS], high_part(row)
                found = jnp.concatenate([select_eight(part[:128], high), select_four(part[128:], high)], axis=0)
                send_a[n * 8 + half * 4 + i] = found.astype(jnp.bfloat16)

    hear(1)
    tell(2)

    @pl.loop(1, YL)
    def _(i):
        other, device = plane_peer(i)
        send(send_a.at[other], recv_a.at[yl], 0, device)

    recv_a[yl] = send_a[yl]
    hear(2)
    tell(3)
    for load in loads[2:]:
        load.wait()
    wait(recv_a.at[pl.ds(0, YL - 1)], arrived.at[0])

    for a in range(YL):
        mixed[pl.ds(a * FP, F), :] = recv_a[a].astype(jnp.float32)
    swap_fields(mixed, table, turned)
    for c in range(Z):
        for q in range(F // 4):
            send_b[c, q] = table[pl.ds(c * FP + 4 * q, 4), :].astype(jnp.bfloat16)

    hear(3)
    for i in FAR_FIRST:
        other, device = column_peer(i)
        send(send_b.at[other], recv_b.at[z], 1, device)

    recv_b[z] = send_b[z]

    @pl.loop(0, ABLK)
    def _(b):
        near = neighbours[:, pl.ds(pl.multiple_of(b * BS, BS), BS)]
        columns[b] = one_hot(ranks, [near[j : j + 1] for j in range(NB)])

    wait(recv_b.at[pl.ds(0, Z - 1)], arrived.at[1])
    for h in range(Z):
        for q in range(F // 4):
            table[pl.ds(h * FP + 4 * q, 4), :] = recv_b[h, q].astype(jnp.float32)
    fill_pairs(pairs, table)

    def reconstruct(b, first, rows, select, recon):
        lanes = pl.ds(pl.multiple_of(b * BS, BS), BS)
        near, along_x, along_y = neighbours[:, lanes], coef_x[:, lanes], coef_y[:, lanes]
        value = table[pl.ds(b * FP + first, rows), :]
        product = multiply(pairs[16 * first : 16 * (first + rows), :], columns[b])
        nearby = [
            select(product[:, j * BS : (j + 1) * BS], high_part(near[j : j + 1])) for j in range(NB)
        ]
        for m, term in enumerate(gradients(value, nearby, along_x, along_y)):
            recon[b, m] = term.astype(jnp.bfloat16)

    def send_blocks(recon, outgoing, incoming, phase):
        def gather_blocks(other):
            for k in range(CAP):
                outgoing[other, k] = recon[send_list[0, k, other]]

        @pl.loop(1, L)
        def _(i):
            other = (member + i) % L
            gather_blocks(other)
            send(
                outgoing.at[other],
                incoming.at[pl.ds(member * CAP, CAP)],
                phase,
                {"region": region, "local": other},
            )

        gather_blocks(member)
        for k in range(CAP):
            incoming[member * CAP + k] = outgoing[member, k]

    @pl.loop(0, 8)
    def _(n):
        for i in range(4):
            reconstruct(n * 4 + i, 0, 8, select_eight, recon_8)

    send_blocks(recon_8, send_c, recv_c, 2)

    @pl.loop(0, 8)
    def _(n):
        for i in range(4):
            reconstruct(n * 4 + i, 8, 4, select_four, recon_4)

    send_blocks(recon_4, send_f, recv_f, 5)
    wait(recv_c.at[pl.ds(0, (L - 1) * CAP)], arrived.at[2])
    wait(recv_f.at[pl.ds(0, (L - 1) * CAP)], arrived.at[5])

    for o in range(OBLK):
        total = jnp.zeros((FP, BS), jnp.float32)
        for k in range(K):
            eight, four = recv_c[cover[o, k]], recv_f[cover[o, k]]
            part = jnp.zeros((FP, BS), jnp.float32)
            for m in range(3):
                fields = [eight[m].astype(jnp.float32), four[m].astype(jnp.float32)]
                chosen = jnp.concatenate(fields + [jnp.zeros((4, BS), jnp.float32)], axis=0)
                part += lax.dot_general(
                    chosen.astype(jnp.bfloat16),
                    weights[(o * K + k) * 3 + m],
                    (((1,), (1,)), ((), ())),
                    preferred_element_type=jnp.float32,
                )
            live = jnp.minimum(jnp.maximum(cover_count[o] - k, 0), 1).astype(jnp.float32)
            total += part * live
        remapped[pl.ds(o * FP, FP), :] = total

    lane = lax.broadcasted_iota(jnp.int32, (8, BS), 1)
    row = lax.broadcasted_iota(jnp.int32, (8, BS), 0)
    for q in range(4):
        cells = pick(spread(ocean_map[:, q * BS : (q + 1) * BS]), row * 16 + (lane & 15))
        block, within = cells >> 7, cells & 127
        for a in range(2):
            total = jnp.zeros((8, BS), jnp.float32)
            for b in range(min(8, F - 8 * a)):
                value = jnp.zeros((8, BS), jnp.float32)
                for o in range(OBLK):
                    near = pick(spread(remapped[pl.ds(o * FP + 8 * a + b, 1), :]), within)
                    value = jnp.where(block == o, near, value)
                total = jnp.where((lane >> 4) == b, value, total)
            for s in range(8):
                send_d[q * 8 + s, :, a * BS : (a + 1) * BS] = total[s : s + 1, :]

    for i in FAR_FIRST:
        other, device = column_peer(i)
        send(send_d.at[other], recv_e.at[y, z], 3, device)

    recv_e[y, z] = send_d[z]
    wait(send_d.at[pl.ds(0, Z - 1)], arrived.at[3])

    @pl.loop(1, Y)
    def _(i):
        other = (y + i) % Y
        send(recv_e.at[y], recv_e.at[y], 4, {"region": z * Y + other, "local": member})

    wait(recv_e.at[pl.ds(0, Y - 1)], arrived.at[4])
    for s in range(Y):
        for t in range(Z):
            landed[pl.ds(s * Z + t, 1), :] = recv_e[s, t]
    for a in range(2):
        turned_out[a] = landed[:, a * BS : (a + 1) * BS].T
        rows = [turned_out[a, pl.ds(y * 4 + p, 8, stride=16), :] for p in range(4)]
        height = min(8, F - 8 * a)
        for c in range(4):
            index = ((lane >> 2) & 3) * 32 + c * 8 + (lane >> 4)
            total = pick(rows[0], index)
            for p in range(1, 4):
                total = jnp.where((lane & 3) == p, pick(rows[p], index), total)
            out[pl.ds(a * 8, height), c * BS : (c + 1) * BS] = total[:height]

    wait(send_a.at[pl.ds(0, YL - 1)], sent.at[0])
    wait(send_b.at[pl.ds(0, Z - 1)], sent.at[1])
    wait(send_c.at[pl.ds(0, L - 1)], sent.at[2])
    wait(send_f.at[pl.ds(0, L - 1)], sent.at[5])
    wait(send_d.at[pl.ds(0, Z - 1)], sent.at[3])
    wait(recv_e.at[pl.ds(0, Y - 1)], sent.at[4])


def shards(
    atm_flux,
    cell_map,
    neighbours,
    coef_x,
    coef_y,
    send_list,
    cover,
    cover_count,
    weights,
    ocean_map,
):
    vmem = pl.BlockSpec(memory_space=pltpu.VMEM)
    blocks = weights.reshape(OBLK * K * 3, BS, BS)
    f32, bf16 = jnp.float32, jnp.bfloat16
    return pl.pallas_call(
        kernel,
        out_shape=jax.ShapeDtypeStruct((F, OBLK * BS), f32),
        in_specs=[pl.BlockSpec(memory_space=pltpu.HBM)] * 10,
        out_specs=vmem,
        scratch_shapes=[
            pltpu.VMEM(atm_flux.shape, bf16),
            pltpu.VMEM(cell_map.shape, jnp.int32),
            pltpu.VMEM(neighbours.shape, jnp.int32),
            pltpu.VMEM(coef_x.shape, f32),
            pltpu.VMEM(coef_y.shape, f32),
            pltpu.SMEM((1, CAP, L), jnp.int32),
            pltpu.SMEM(cover.shape, jnp.int32),
            pltpu.SMEM(cover_count.shape, jnp.int32),
            pltpu.VMEM(blocks.shape, bf16),
            pltpu.VMEM(ocean_map.shape, jnp.int32),
            pltpu.VMEM((256, BS), bf16),
            pltpu.VMEM((ABLK, 256, NB * BS), bf16),
            pltpu.VMEM((16 * F, 2 * BS), bf16),
            pltpu.VMEM((32 * FP, BS), f32),
            pltpu.VMEM((32 * FP, BS), f32),
            pltpu.VMEM((F // 4, BS, BS), f32),
            pltpu.VMEM((32, BS), jnp.int32),
            pltpu.VMEM((ABLK, 3, 8, BS), bf16),
            pltpu.VMEM((ABLK, 3, 4, BS), bf16),
            pltpu.VMEM((OBLK * FP, BS), f32),
            pltpu.VMEM((Y * Z, 2 * BS), f32),
            pltpu.VMEM((2, BS, BS), f32),
            pltpu.VMEM((YL, F, BS), bf16),
            pltpu.VMEM((YL, F, BS), bf16),
            pltpu.VMEM((Z, F // 4, 4, BS), bf16),
            pltpu.VMEM((Z, F // 4, 4, BS), bf16),
            pltpu.VMEM((L, CAP, 3, 8, BS), bf16),
            pltpu.VMEM((L * CAP, 3, 8, BS), bf16),
            pltpu.VMEM((L, CAP, 3, 4, BS), bf16),
            pltpu.VMEM((L * CAP, 3, 4, BS), bf16),
            pltpu.VMEM((Z, 1, 2 * BS), f32),
            pltpu.VMEM((Y, Z, 1, 2 * BS), f32),
            pltpu.SemaphoreType.DMA((10,)),
            pltpu.SemaphoreType.DMA((6,)),
            pltpu.SemaphoreType.DMA((6,)),
            pltpu.SemaphoreType.REGULAR((4,)),
        ],
        compiler_params=pltpu.CompilerParams(
            collective_id=0, has_side_effects=True, vmem_limit_bytes=62 * 2**20
        ),
    )(
        atm_flux,
        cell_map,
        neighbours,
        coef_x,
        coef_y,
        jnp.swapaxes(send_list, 1, 2),
        cover,
        cover_count,
        blocks,
        ocean_map,
    )


def solution(mesh):
    return jax.shard_map(
        shards,
        mesh=mesh,
        in_specs=(
            P(None, ("region", "local")),
            P(("region", "local"), None),
            P(None, ("region", "local")),
            P(None, ("region", "local")),
            P(None, ("region", "local")),
            P(("region", "local"), None, None),
            P(("region", "local"), None),
            P(("region", "local")),
            P(("region", "local"), None, None, None, None),
            P(("region", "local"), None),
        ),
        out_specs=P(None, ("region", "local")),
        check_vma=False,
    )
```

```python
import jax
import jax.numpy as jnp
from jax import lax
from jax.experimental import pallas as pl
from jax.experimental.pallas import tpu as pltpu
from jax.sharding import PartitionSpec as P

MESH = pl.DeviceIdType.MESH
F = 12
FP = 16
Z, Y, L = 32, 4, 8
YL = Y * L
NB = 4
K = 4
CAP = 4
OBLK = 4
BS = 128
ABLK = 32
NEAR = Z // 4
FAR_FIRST = sorted(range(1, Z), key=lambda i: -min(i, Z - i))


def pick(table, index):
    return jnp.take_along_axis(table, index, axis=1, mode="promise_in_bounds")


def spread(row):
    return jnp.broadcast_to(row, (8, BS))


def swap_blocks(parts, turned):
    lane = lax.broadcasted_iota(jnp.int32, (32, BS), 1)
    turned[...] = jnp.concatenate(parts, axis=0).T
    rows = [turned[pl.ds(g, 32, stride=4), :] for g in range(4)]
    result = []
    for i in range(len(parts)):
        index = i * 32 + (lane >> 2)
        total = pick(rows[0], index)
        for g in range(1, 4):
            total = jnp.where((lane & 3) == g, pick(rows[g], index), total)
        result.append(total)
    return result


def swap_fields(source, target, turned):
    for q in range(F // 4):
        parts = [source[pl.ds(4 * q + i, 32, stride=FP), :] for i in range(4)]
        for i, part in enumerate(swap_blocks(parts, turned.at[q])):
            target[pl.ds(4 * q + i, 32, stride=FP), :] = part


def one_hot(ranks, rows):
    columns = []
    for row in rows:
        low = jnp.broadcast_to((row & 255).astype(jnp.float32), (16, BS)).astype(jnp.bfloat16)
        low = jnp.broadcast_to(low[None], (16, 16, BS)).reshape(256, BS)
        one, zero = jnp.ones((256, BS), jnp.bfloat16), jnp.zeros((256, BS), jnp.bfloat16)
        columns.append(jnp.where(ranks[...] == low, one, zero))
    return jnp.concatenate(columns, axis=1)


def fill_pairs(pairs, table):
    for parity in range(2):
        lanes = slice(parity * BS, (parity + 1) * BS)
        starts = [(2 * h + parity) * FP for h in range(16)]
        for p in range(8):
            rows = [table[pl.ds(start, 8), :] for start in starts[2 * p : 2 * p + 2]]
            pairs[pl.ds(16 * p, 16), lanes] = jnp.concatenate(rows, axis=0).astype(jnp.bfloat16)
        for p in range(4):
            rows = [table[pl.ds(start + 8, 4), :] for start in starts[4 * p : 4 * p + 4]]
            pairs[pl.ds(128 + 16 * p, 16), lanes] = jnp.concatenate(rows, axis=0).astype(jnp.bfloat16)


def high_part(row):
    return jnp.broadcast_to(row >> 8, (8, BS))


def select_eight(product, high):
    value = product[:8]
    for h in range(1, 16):
        value = jnp.where(high == h, product[8 * h : 8 * h + 8], value)
    return value


def select_four(product, high):
    own = high - (lax.broadcasted_iota(jnp.int32, (8, BS), 0) >> 2)
    value = jnp.zeros((8, BS), jnp.float32)
    for p in range(8):
        value = jnp.where(own == 2 * p, product[8 * p : 8 * p + 8], value)
    return value[:4] + value[4:]


def multiply(table, columns):
    return jnp.dot(table, columns, preferred_element_type=jnp.float32)


def gradients(value, nearby, along_x, along_y):
    change = [found - value for found in nearby]
    slope_x = sum(along_x[j : j + 1] * change[j] for j in range(NB))
    slope_y = sum(along_y[j : j + 1] * change[j] for j in range(NB))
    upper, lower = value, value
    for found in nearby:
        upper, lower = jnp.maximum(upper, found), jnp.minimum(lower, found)
    steep = jnp.abs(slope_x) + jnp.abs(slope_y)
    factor = jnp.minimum(1.0, (upper - lower) / jnp.maximum(steep, 1.0))
    return factor * slope_x, factor * slope_y


def kernel(
    atm_hbm,
    cell_map_hbm,
    neighbours_hbm,
    coef_x_hbm,
    coef_y_hbm,
    send_list_hbm,
    cover_hbm,
    cover_count_hbm,
    weights_hbm,
    ocean_map_hbm,
    out,
    atm,
    cell_map,
    neighbours,
    coef_x,
    coef_y,
    send_list,
    cover,
    cover_count,
    weights,
    ocean_map,
    ranks,
    columns,
    pairs,
    table,
    mixed,
    turned,
    map_rows,
    recon_8,
    recon_4,
    remapped,
    landed,
    turned_out,
    send_a,
    recv_a,
    send_b,
    recv_b,
    send_c,
    recv_c,
    send_f,
    recv_f,
    send_v,
    recv_v,
    send_d,
    recv_e,
    loaded,
    sent,
    arrived,
    reach,
):
    region, member = lax.axis_index("region"), lax.axis_index("local")
    z, y = region // Y, region % Y
    yl = y * L + member

    def plane_peer(i):
        other = (yl + i) % YL
        return other, {"region": z * Y + other // L, "local": other % L}

    def column_peer(i):
        other = (z + i) % Z
        return other, {"region": other * Y + y, "local": member}

    def send(source, target, phase, device):
        pltpu.make_async_remote_copy(
            src_ref=source,
            dst_ref=target,
            send_sem=sent.at[phase],
            recv_sem=arrived.at[phase],
            device_id=device,
            device_id_type=MESH,
        ).start()

    def wait(buffer, semaphore):
        pltpu.make_async_copy(buffer, buffer, semaphore).wait()

    loads = [
        pltpu.make_async_copy(source, target, loaded.at[i])
        for i, (source, target) in enumerate(
            (
                (cell_map_hbm, cell_map),
                (atm_hbm, atm),
                (neighbours_hbm, neighbours),
                (coef_x_hbm, coef_x),
                (coef_y_hbm, coef_y),
                (send_list_hbm, send_list),
                (cover_hbm, cover),
                (cover_count_hbm, cover_count),
                (ocean_map_hbm, ocean_map),
                (weights_hbm, weights),
            )
        )
    ]
    barrier = pltpu.get_barrier_semaphore()

    for i in sorted(range(1, NEAR + 1), reverse=True):
        for j in (i, Z - i):
            pl.semaphore_signal(barrier, inc=1, device_id=column_peer(j)[1], device_id_type=MESH)

    for load in loads[:2]:
        load.start()

    @pl.loop(1, YL)
    def _(i):
        pl.semaphore_signal(barrier, inc=1, device_id=plane_peer(i)[1], device_id_type=MESH)

    for load in loads[2:]:
        load.start()

    ranks[...] = lax.broadcasted_iota(jnp.int32, (256, BS), 0).astype(jnp.float32).astype(jnp.bfloat16)
    for load in loads[:2]:
        load.wait()
    for h in range(32):
        lanes = slice(h * BS, (h + 1) * BS)
        table[pl.ds(h * FP, F), :] = atm[:, lanes].astype(jnp.float32)
        map_rows[pl.ds(h, 1), :] = cell_map[:, lanes]
    fill_pairs(pairs, table)
    cells = map_rows[...].astype(jnp.float32)
    map_rows[...] = swap_blocks([cells] * 4, turned.at[0])[0].astype(jnp.int32)

    @pl.loop(0, YL // 8)
    def _(n):
        for half in range(2):
            rows = [map_rows[pl.ds(n * 8 + half * 4 + i, 1), :] for i in range(4)]
            product = multiply(pairs[...], one_hot(ranks, rows))
            for i, row in enumerate(rows):
                part, high = product[:, i * BS : (i + 1) * BS], high_part(row)
                found = jnp.concatenate([select_eight(part[:128], high), select_four(part[128:], high)], axis=0)
                send_a[n * 8 + half * 4 + i] = found.astype(jnp.bfloat16)

    pl.semaphore_wait(barrier, YL - 1 + 2 * NEAR)
    for j in (NEAR, Z - NEAR):
        pl.semaphore_signal(reach, inc=1, device_id=column_peer(j)[1], device_id_type=MESH)


    @pl.loop(1, YL)
    def _(i):
        other, device = plane_peer(i)
        send(send_a.at[other], recv_a.at[yl], 0, device)

    recv_a[yl] = send_a[yl]
    for load in loads[2:]:
        load.wait()
    wait(recv_a.at[pl.ds(0, YL - 1)], arrived.at[0])

    for a in range(YL):
        mixed[pl.ds(a * FP, F), :] = recv_a[a].astype(jnp.float32)
    swap_fields(mixed, table, turned)
    for c in range(Z):
        for q in range(F // 4):
            send_b[c, q] = table[pl.ds(c * FP + 4 * q, 4), :].astype(jnp.bfloat16)

    pl.semaphore_wait(reach, 2)
    for i in FAR_FIRST:
        other, device = column_peer(i)
        send(send_b.at[other], recv_b.at[z], 1, device)

    recv_b[z] = send_b[z]

    @pl.loop(0, ABLK)
    def _(b):
        near = neighbours[:, pl.ds(pl.multiple_of(b * BS, BS), BS)]
        columns[b] = one_hot(ranks, [near[j : j + 1] for j in range(NB)])

    wait(recv_b.at[pl.ds(0, Z - 1)], arrived.at[1])
    def send_blocks(*groups):
        def gather_blocks(other):
            for blocks, outgoing, _, _ in groups:
                for k in range(CAP):
                    outgoing[other, k] = blocks[send_list[0, k, other]]

        @pl.loop(1, L)
        def _(i):
            other = (member + i) % L
            gather_blocks(other)
            for _, outgoing, incoming, phase in groups:
                send(
                    outgoing.at[other],
                    incoming.at[pl.ds(member * CAP, CAP)],
                    phase,
                    {"region": region, "local": other},
                )

        gather_blocks(member)
        for _, outgoing, incoming, _ in groups:
            for k in range(CAP):
                incoming[member * CAP + k] = outgoing[member, k]

    send_blocks((recv_b, send_v, recv_v, 6))

    for h in range(Z):
        for q in range(F // 4):
            table[pl.ds(h * FP + 4 * q, 4), :] = recv_b[h, q].astype(jnp.float32)
    fill_pairs(pairs, table)

    def reconstruct(b):
        lanes = pl.ds(pl.multiple_of(b * BS, BS), BS)
        near, along_x, along_y = neighbours[:, lanes], coef_x[:, lanes], coef_y[:, lanes]
        high = [high_part(near[j : j + 1]) for j in range(NB)]
        product = multiply(pairs[...], columns[b])
        parts = [product[:, j * BS : (j + 1) * BS] for j in range(NB)]
        eight = [select_eight(parts[j][:128], high[j]) for j in range(NB)]
        four = [select_four(parts[j][128:], high[j]) for j in range(NB)]
        for nearby, first, rows, recon in ((eight, 0, 8, recon_8), (four, 8, 4, recon_4)):
            value = table[pl.ds(b * FP + first, rows), :]
            for m, term in enumerate(gradients(value, nearby, along_x, along_y)):
                recon[b, m] = term.astype(jnp.bfloat16)

    @pl.loop(0, 4)
    def _(n):
        for i in range(8):
            reconstruct(n * 8 + i)

    send_blocks((recon_8, send_c, recv_c, 2), (recon_4, send_f, recv_f, 5))
    wait(recv_v.at[pl.ds(0, (L - 1) * CAP)], arrived.at[6])
    wait(recv_c.at[pl.ds(0, (L - 1) * CAP)], arrived.at[2])
    wait(recv_f.at[pl.ds(0, (L - 1) * CAP)], arrived.at[5])

    for o in range(OBLK):
        total = jnp.zeros((FP, BS), jnp.float32)
        for k in range(K):
            slot = cover[o, k]
            values, eight, four = recv_v[slot], recv_c[slot], recv_f[slot]
            fields = [[values[q] for q in range(F // 4)]]
            fields += [[eight[m], four[m]] for m in range(2)]
            part = jnp.zeros((FP, BS), jnp.float32)
            for m in range(3):
                rows = [rows.astype(jnp.float32) for rows in fields[m]]
                chosen = jnp.concatenate(rows + [jnp.zeros((FP - F, BS), jnp.float32)], axis=0)
                part += lax.dot_general(
                    chosen.astype(jnp.bfloat16),
                    weights[(o * K + k) * 3 + m],
                    (((1,), (1,)), ((), ())),
                    preferred_element_type=jnp.float32,
                )
            live = jnp.minimum(jnp.maximum(cover_count[o] - k, 0), 1).astype(jnp.float32)
            total += part * live
        remapped[pl.ds(o * FP, FP), :] = total

    lane = lax.broadcasted_iota(jnp.int32, (8, BS), 1)
    row = lax.broadcasted_iota(jnp.int32, (8, BS), 0)
    for q in range(4):
        cells = pick(spread(ocean_map[:, q * BS : (q + 1) * BS]), row * 16 + (lane & 15))
        block, within = cells >> 7, cells & 127
        for a in range(2):
            total = jnp.zeros((8, BS), jnp.float32)
            for b in range(min(8, F - 8 * a)):
                value = jnp.zeros((8, BS), jnp.float32)
                for o in range(OBLK):
                    near = pick(spread(remapped[pl.ds(o * FP + 8 * a + b, 1), :]), within)
                    value = jnp.where(block == o, near, value)
                total = jnp.where((lane >> 4) == b, value, total)
            for s in range(8):
                send_d[q * 8 + s, :, a * BS : (a + 1) * BS] = total[s : s + 1, :]

    for i in FAR_FIRST:
        other, device = column_peer(i)
        send(send_d.at[other], recv_e.at[y, z], 3, device)

    recv_e[y, z] = send_d[z]
    wait(send_d.at[pl.ds(0, Z - 1)], arrived.at[3])

    @pl.loop(1, Y)
    def _(i):
        other = (y + i) % Y
        send(recv_e.at[y], recv_e.at[y], 4, {"region": z * Y + other, "local": member})

    wait(recv_e.at[pl.ds(0, Y - 1)], arrived.at[4])
    for s in range(Y):
        for t in range(Z):
            landed[pl.ds(s * Z + t, 1), :] = recv_e[s, t]
    for a in range(2):
        turned_out[a] = landed[:, a * BS : (a + 1) * BS].T
        rows = [turned_out[a, pl.ds(y * 4 + p, 8, stride=16), :] for p in range(4)]
        height = min(8, F - 8 * a)
        for c in range(4):
            index = ((lane >> 2) & 3) * 32 + c * 8 + (lane >> 4)
            total = pick(rows[0], index)
            for p in range(1, 4):
                total = jnp.where((lane & 3) == p, pick(rows[p], index), total)
            out[pl.ds(a * 8, height), c * BS : (c + 1) * BS] = total[:height]

    wait(send_a.at[pl.ds(0, YL - 1)], sent.at[0])
    wait(send_b.at[pl.ds(0, Z - 1)], sent.at[1])
    wait(send_c.at[pl.ds(0, L - 1)], sent.at[2])
    wait(send_f.at[pl.ds(0, L - 1)], sent.at[5])
    wait(send_v.at[pl.ds(0, L - 1)], sent.at[6])
    wait(send_d.at[pl.ds(0, Z - 1)], sent.at[3])
    wait(recv_e.at[pl.ds(0, Y - 1)], sent.at[4])


def shards(
    atm_flux,
    cell_map,
    neighbours,
    coef_x,
    coef_y,
    send_list,
    cover,
    cover_count,
    weights,
    ocean_map,
):
    vmem = pl.BlockSpec(memory_space=pltpu.VMEM)
    blocks = weights.reshape(OBLK * K * 3, BS, BS)
    f32, bf16 = jnp.float32, jnp.bfloat16
    return pl.pallas_call(
        kernel,
        out_shape=jax.ShapeDtypeStruct((F, OBLK * BS), f32),
        in_specs=[pl.BlockSpec(memory_space=pltpu.HBM)] * 10,
        out_specs=vmem,
        scratch_shapes=[
            pltpu.VMEM(atm_flux.shape, bf16),
            pltpu.VMEM(cell_map.shape, jnp.int32),
            pltpu.VMEM(neighbours.shape, jnp.int32),
            pltpu.VMEM(coef_x.shape, f32),
            pltpu.VMEM(coef_y.shape, f32),
            pltpu.SMEM((1, CAP, L), jnp.int32),
            pltpu.SMEM(cover.shape, jnp.int32),
            pltpu.SMEM(cover_count.shape, jnp.int32),
            pltpu.VMEM(blocks.shape, bf16),
            pltpu.VMEM(ocean_map.shape, jnp.int32),
            pltpu.VMEM((256, BS), bf16),
            pltpu.VMEM((ABLK, 256, NB * BS), bf16),
            pltpu.VMEM((16 * F, 2 * BS), bf16),
            pltpu.VMEM((32 * FP, BS), f32),
            pltpu.VMEM((32 * FP, BS), f32),
            pltpu.VMEM((F // 4, BS, BS), f32),
            pltpu.VMEM((32, BS), jnp.int32),
            pltpu.VMEM((ABLK, 2, 8, BS), bf16),
            pltpu.VMEM((ABLK, 2, 4, BS), bf16),
            pltpu.VMEM((OBLK * FP, BS), f32),
            pltpu.VMEM((Y * Z, 2 * BS), f32),
            pltpu.VMEM((2, BS, BS), f32),
            pltpu.VMEM((YL, F, BS), bf16),
            pltpu.VMEM((YL, F, BS), bf16),
            pltpu.VMEM((Z, F // 4, 4, BS), bf16),
            pltpu.VMEM((Z, F // 4, 4, BS), bf16),
            pltpu.VMEM((L, CAP, 2, 8, BS), bf16),
            pltpu.VMEM((L * CAP, 2, 8, BS), bf16),
            pltpu.VMEM((L, CAP, 2, 4, BS), bf16),
            pltpu.VMEM((L * CAP, 2, 4, BS), bf16),
            pltpu.VMEM((L, CAP, F // 4, 4, BS), bf16),
            pltpu.VMEM((L * CAP, F // 4, 4, BS), bf16),
            pltpu.VMEM((Z, 1, 2 * BS), f32),
            pltpu.VMEM((Y, Z, 1, 2 * BS), f32),
            pltpu.SemaphoreType.DMA((10,)),
            pltpu.SemaphoreType.DMA((7,)),
            pltpu.SemaphoreType.DMA((7,)),
            pltpu.SemaphoreType.REGULAR,
        ],
        compiler_params=pltpu.CompilerParams(
            collective_id=0, has_side_effects=True, vmem_limit_bytes=62 * 2**20
        ),
    )(
        atm_flux,
        cell_map,
        neighbours,
        coef_x,
        coef_y,
        jnp.swapaxes(send_list, 1, 2),
        cover,
        cover_count,
        blocks,
        ocean_map,
    )


def solution(mesh):
    return jax.shard_map(
        shards,
        mesh=mesh,
        in_specs=(
            P(None, ("region", "local")),
            P(("region", "local"), None),
            P(None, ("region", "local")),
            P(None, ("region", "local")),
            P(None, ("region", "local")),
            P(("region", "local"), None, None),
            P(("region", "local"), None),
            P(("region", "local")),
            P(("region", "local"), None, None, None, None),
            P(("region", "local"), None),
        ),
        out_specs=P(None, ("region", "local")),
        check_vma=False,
    )
```

```python
import jax
import jax.numpy as jnp
from jax import lax
from jax.experimental import pallas as pl
from jax.experimental.pallas import tpu as pltpu
from jax.sharding import PartitionSpec as P

MESH = pl.DeviceIdType.MESH
F = 12
FP = 16
Z, Y, L = 32, 4, 8
YL = Y * L
NB = 4
K = 4
CAP = 4
OBLK = 4
BS = 128
ABLK = 32
NEAR = Z // 4
FAR_FIRST = sorted(range(1, Z), key=lambda i: -min(i, Z - i))


def pick(table, index):
    return jnp.take_along_axis(table, index, axis=1, mode="promise_in_bounds")


def spread(row):
    return jnp.broadcast_to(row, (8, BS))


def swap_blocks(parts, turned):
    lane = lax.broadcasted_iota(jnp.int32, (32, BS), 1)
    turned[...] = jnp.concatenate(parts, axis=0).T
    rows = [turned[pl.ds(g, 32, stride=4), :] for g in range(4)]
    result = []
    for i in range(len(parts)):
        index = i * 32 + (lane >> 2)
        total = pick(rows[0], index)
        for g in range(1, 4):
            total = jnp.where((lane & 3) == g, pick(rows[g], index), total)
        result.append(total)
    return result


def swap_fields(source, target, turned):
    for q in range(F // 4):
        parts = [source[pl.ds(4 * q + i, 32, stride=FP), :] for i in range(4)]
        for i, part in enumerate(swap_blocks(parts, turned.at[q])):
            target[pl.ds(4 * q + i, 32, stride=FP), :] = part


def one_hot(ranks, rows):
    columns = []
    for row in rows:
        low = jnp.broadcast_to((row & 255).astype(jnp.float32), (16, BS)).astype(jnp.bfloat16)
        low = jnp.broadcast_to(low[None], (16, 16, BS)).reshape(256, BS)
        one, zero = jnp.ones((256, BS), jnp.bfloat16), jnp.zeros((256, BS), jnp.bfloat16)
        columns.append(jnp.where(ranks[...] == low, one, zero))
    return jnp.concatenate(columns, axis=1)


def fill_pairs(pairs, table):
    for parity in range(2):
        lanes = slice(parity * BS, (parity + 1) * BS)
        starts = [(2 * h + parity) * FP for h in range(16)]
        for p in range(8):
            rows = [table[pl.ds(start, 8), :] for start in starts[2 * p : 2 * p + 2]]
            pairs[pl.ds(16 * p, 16), lanes] = jnp.concatenate(rows, axis=0).astype(jnp.bfloat16)
        for p in range(4):
            rows = [table[pl.ds(start + 8, 4), :] for start in starts[4 * p : 4 * p + 4]]
            pairs[pl.ds(128 + 16 * p, 16), lanes] = jnp.concatenate(rows, axis=0).astype(jnp.bfloat16)


def high_part(row):
    return jnp.broadcast_to(row >> 8, (8, BS))


def select_eight(product, high):
    value = product[:8]
    for h in range(1, 16):
        value = jnp.where(high == h, product[8 * h : 8 * h + 8], value)
    return value


def select_four(product, high):
    own = high - (lax.broadcasted_iota(jnp.int32, (8, BS), 0) >> 2)
    value = jnp.zeros((8, BS), jnp.float32)
    for p in range(8):
        value = jnp.where(own == 2 * p, product[8 * p : 8 * p + 8], value)
    return value[:4] + value[4:]


def multiply(table, columns):
    return jnp.dot(table, columns, preferred_element_type=jnp.float32)


def gradients(value, nearby, along_x, along_y):
    change = [found - value for found in nearby]
    slope_x = sum(along_x[j : j + 1] * change[j] for j in range(NB))
    slope_y = sum(along_y[j : j + 1] * change[j] for j in range(NB))
    upper, lower = value, value
    for found in nearby:
        upper, lower = jnp.maximum(upper, found), jnp.minimum(lower, found)
    steep = jnp.abs(slope_x) + jnp.abs(slope_y)
    factor = jnp.minimum(1.0, (upper - lower) / jnp.maximum(steep, 1.0))
    return factor * slope_x, factor * slope_y


def kernel(
    atm_hbm,
    cell_map_hbm,
    neighbours_hbm,
    coef_x_hbm,
    coef_y_hbm,
    send_list_hbm,
    cover_hbm,
    cover_count_hbm,
    weights_hbm,
    ocean_map_hbm,
    out,
    atm,
    cell_map,
    neighbours,
    coef_x,
    coef_y,
    send_list,
    cover,
    cover_count,
    weights,
    ocean_map,
    ranks,
    columns,
    pairs,
    table,
    mixed,
    turned,
    map_rows,
    recon_8,
    recon_4,
    remapped,
    landed,
    turned_out,
    send_a,
    recv_a,
    send_b,
    recv_b,
    send_c,
    recv_c,
    send_f,
    recv_f,
    send_v,
    recv_v,
    send_d,
    recv_e,
    loaded,
    sent,
    arrived,
    reach,
):
    region, member = lax.axis_index("region"), lax.axis_index("local")
    z, y = region // Y, region % Y
    yl = y * L + member

    def plane_peer(i):
        other = (yl + i) % YL
        return other, {"region": z * Y + other // L, "local": other % L}

    def column_peer(i):
        other = (z + i) % Z
        return other, {"region": other * Y + y, "local": member}

    def send(source, target, phase, device):
        pltpu.make_async_remote_copy(
            src_ref=source,
            dst_ref=target,
            send_sem=sent.at[phase],
            recv_sem=arrived.at[phase],
            device_id=device,
            device_id_type=MESH,
        ).start()

    def wait(buffer, semaphore):
        pltpu.make_async_copy(buffer, buffer, semaphore).wait()

    loads = [
        pltpu.make_async_copy(source, target, loaded.at[i])
        for i, (source, target) in enumerate(
            (
                (cell_map_hbm, cell_map),
                (atm_hbm, atm),
                (neighbours_hbm, neighbours),
                (coef_x_hbm, coef_x),
                (coef_y_hbm, coef_y),
                (send_list_hbm, send_list),
                (cover_hbm, cover),
                (cover_count_hbm, cover_count),
                (ocean_map_hbm, ocean_map),
                (weights_hbm, weights),
            )
        )
    ]
    barrier = pltpu.get_barrier_semaphore()

    for i in sorted(range(1, NEAR + 1), reverse=True):
        for j in (i, Z - i):
            pl.semaphore_signal(barrier, inc=1, device_id=column_peer(j)[1], device_id_type=MESH)

    for load in loads[:2]:
        load.start()

    @pl.loop(1, YL)
    def _(i):
        pl.semaphore_signal(barrier, inc=1, device_id=plane_peer(i)[1], device_id_type=MESH)

    for load in loads[2:]:
        load.start()

    ranks[...] = lax.broadcasted_iota(jnp.int32, (256, BS), 0).astype(jnp.float32).astype(jnp.bfloat16)
    for load in loads[:2]:
        load.wait()
    for h in range(32):
        lanes = slice(h * BS, (h + 1) * BS)
        table[pl.ds(h * FP, F), :] = atm[:, lanes].astype(jnp.float32)
        map_rows[pl.ds(h, 1), :] = cell_map[:, lanes]
    fill_pairs(pairs, table)
    cells = map_rows[...].astype(jnp.float32)
    map_rows[...] = swap_blocks([cells] * 4, turned.at[0])[0].astype(jnp.int32)

    @pl.loop(0, YL // 8)
    def _(n):
        for half in range(2):
            rows = [map_rows[pl.ds(n * 8 + half * 4 + i, 1), :] for i in range(4)]
            product = multiply(pairs[...], one_hot(ranks, rows))
            for i, row in enumerate(rows):
                part, high = product[:, i * BS : (i + 1) * BS], high_part(row)
                found = jnp.concatenate([select_eight(part[:128], high), select_four(part[128:], high)], axis=0)
                send_a[n * 8 + half * 4 + i] = found.astype(jnp.bfloat16)

    pl.semaphore_wait(barrier, YL - 1 + 2 * NEAR)
    for j in (NEAR, Z - NEAR):
        pl.semaphore_signal(reach, inc=1, device_id=column_peer(j)[1], device_id_type=MESH)


    @pl.loop(1, YL)
    def _(i):
        other, device = plane_peer(i)
        send(send_a.at[other], recv_a.at[yl], 0, device)

    recv_a[yl] = send_a[yl]
    for load in loads[2:]:
        load.wait()
    wait(recv_a.at[pl.ds(0, YL - 1)], arrived.at[0])

    for a in range(YL):
        mixed[pl.ds(a * FP, F), :] = recv_a[a].astype(jnp.float32)
    swap_fields(mixed, table, turned)
    for c in range(Z):
        for q in range(F // 4):
            send_b[c, q] = table[pl.ds(c * FP + 4 * q, 4), :].astype(jnp.bfloat16)

    pl.semaphore_wait(reach, 2)
    for i in FAR_FIRST:
        other, device = column_peer(i)
        send(send_b.at[other], recv_b.at[z], 1, device)

    recv_b[z] = send_b[z]

    @pl.loop(0, ABLK)
    def _(b):
        near = neighbours[:, pl.ds(pl.multiple_of(b * BS, BS), BS)]
        columns[b] = one_hot(ranks, [near[j : j + 1] for j in range(NB)])

    wait(recv_b.at[pl.ds(0, Z - 1)], arrived.at[1])
    def send_blocks(*groups):
        for other in range(L):
            for k in range(CAP):
                block = send_list[0, k, other]
                for blocks, outgoing, _, _ in groups:
                    outgoing[other, k] = blocks[block]

        for i in range(1, L):
            other = lax.rem(member + i, L)
            for _, outgoing, incoming, phase in groups:
                send(
                    outgoing.at[other],
                    incoming.at[pl.ds(member * CAP, CAP)],
                    phase,
                    {"region": region, "local": other},
                )

        for _, outgoing, incoming, _ in groups:
            for k in range(CAP):
                incoming[member * CAP + k] = outgoing[member, k]

    send_blocks((recv_b, send_v, recv_v, 6))

    for h in range(Z):
        for q in range(F // 4):
            table[pl.ds(h * FP + 4 * q, 4), :] = recv_b[h, q].astype(jnp.float32)
    fill_pairs(pairs, table)

    def reconstruct(b):
        lanes = pl.ds(pl.multiple_of(b * BS, BS), BS)
        near, along_x, along_y = neighbours[:, lanes], coef_x[:, lanes], coef_y[:, lanes]
        high = [high_part(near[j : j + 1]) for j in range(NB)]
        product = multiply(pairs[...], columns[b])
        parts = [product[:, j * BS : (j + 1) * BS] for j in range(NB)]
        eight = [select_eight(parts[j][:128], high[j]) for j in range(NB)]
        four = [select_four(parts[j][128:], high[j]) for j in range(NB)]
        for nearby, first, rows, recon in ((eight, 0, 8, recon_8), (four, 8, 4, recon_4)):
            value = table[pl.ds(b * FP + first, rows), :]
            for m, term in enumerate(gradients(value, nearby, along_x, along_y)):
                recon[b, m] = term.astype(jnp.bfloat16)

    @pl.loop(0, 4)
    def _(n):
        for i in range(8):
            reconstruct(n * 8 + i)

    send_blocks((recon_8, send_c, recv_c, 2), (recon_4, send_f, recv_f, 5))
    wait(recv_v.at[pl.ds(0, (L - 1) * CAP)], arrived.at[6])
    wait(recv_c.at[pl.ds(0, (L - 1) * CAP)], arrived.at[2])
    wait(recv_f.at[pl.ds(0, (L - 1) * CAP)], arrived.at[5])

    for o in range(OBLK):
        total = jnp.zeros((FP, BS), jnp.float32)
        for k in range(K):
            slot = cover[o, k]
            values, eight, four = recv_v[slot], recv_c[slot], recv_f[slot]
            fields = [[values[q] for q in range(F // 4)]]
            fields += [[eight[m], four[m]] for m in range(2)]
            rest = [jnp.zeros((FP - F, BS), jnp.float32)]
            chosen = [
                jnp.concatenate([rows.astype(jnp.float32) for rows in parts] + rest, axis=0)
                for parts in fields
            ]
            part = lax.dot_general(
                jnp.concatenate(chosen, axis=1).astype(jnp.bfloat16),
                jnp.concatenate([weights[(o * K + k) * 3 + m] for m in range(3)], axis=1),
                (((1,), (1,)), ((), ())),
                preferred_element_type=jnp.float32,
            )
            live = jnp.minimum(jnp.maximum(cover_count[o] - k, 0), 1).astype(jnp.float32)
            total += part * live
        remapped[pl.ds(o * FP, FP), :] = total

    lane = lax.broadcasted_iota(jnp.int32, (8, BS), 1)
    row = lax.broadcasted_iota(jnp.int32, (8, BS), 0)
    for q in range(4):
        cells = pick(spread(ocean_map[:, q * BS : (q + 1) * BS]), row * 16 + (lane & 15))
        block, within = cells >> 7, cells & 127
        for a in range(2):
            total = jnp.zeros((8, BS), jnp.float32)
            for b in range(min(8, F - 8 * a)):
                value = jnp.zeros((8, BS), jnp.float32)
                for o in range(OBLK):
                    near = pick(spread(remapped[pl.ds(o * FP + 8 * a + b, 1), :]), within)
                    value = jnp.where(block == o, near, value)
                total = jnp.where((lane >> 4) == b, value, total)
            for s in range(8):
                send_d[q * 8 + s, :, a * BS : (a + 1) * BS] = total[s : s + 1, :]

    for i in FAR_FIRST:
        other, device = column_peer(i)
        send(send_d.at[other], recv_e.at[y, z], 3, device)

    recv_e[y, z] = send_d[z]
    wait(send_d.at[pl.ds(0, Z - 1)], arrived.at[3])

    for i in (2, 1, 3):
        other = (y + i) % Y
        send(recv_e.at[y], recv_e.at[y], 4, {"region": z * Y + other, "local": member})

    wait(recv_e.at[pl.ds(0, Y - 1)], arrived.at[4])
    for s in range(Y):
        for t in range(Z):
            landed[pl.ds(s * Z + t, 1), :] = recv_e[s, t]
    for a in range(2):
        turned_out[a] = landed[:, a * BS : (a + 1) * BS].T
        rows = [turned_out[a, pl.ds(y * 4 + p, 8, stride=16), :] for p in range(4)]
        height = min(8, F - 8 * a)
        for c in range(4):
            index = ((lane >> 2) & 3) * 32 + c * 8 + (lane >> 4)
            total = pick(rows[0], index)
            for p in range(1, 4):
                total = jnp.where((lane & 3) == p, pick(rows[p], index), total)
            out[pl.ds(a * 8, height), c * BS : (c + 1) * BS] = total[:height]

    wait(send_a.at[pl.ds(0, YL - 1)], sent.at[0])
    wait(send_b.at[pl.ds(0, Z - 1)], sent.at[1])
    wait(send_c.at[pl.ds(0, L - 1)], sent.at[2])
    wait(send_f.at[pl.ds(0, L - 1)], sent.at[5])
    wait(send_v.at[pl.ds(0, L - 1)], sent.at[6])
    wait(send_d.at[pl.ds(0, Z - 1)], sent.at[3])
    wait(recv_e.at[pl.ds(0, Y - 1)], sent.at[4])


def shards(
    atm_flux,
    cell_map,
    neighbours,
    coef_x,
    coef_y,
    send_list,
    cover,
    cover_count,
    weights,
    ocean_map,
):
    vmem = pl.BlockSpec(memory_space=pltpu.VMEM)
    blocks = weights.reshape(OBLK * K * 3, BS, BS)
    f32, bf16 = jnp.float32, jnp.bfloat16
    return pl.pallas_call(
        kernel,
        out_shape=jax.ShapeDtypeStruct((F, OBLK * BS), f32),
        in_specs=[pl.BlockSpec(memory_space=pltpu.HBM)] * 10,
        out_specs=vmem,
        scratch_shapes=[
            pltpu.VMEM(atm_flux.shape, bf16),
            pltpu.VMEM(cell_map.shape, jnp.int32),
            pltpu.VMEM(neighbours.shape, jnp.int32),
            pltpu.VMEM(coef_x.shape, f32),
            pltpu.VMEM(coef_y.shape, f32),
            pltpu.SMEM((1, CAP, L), jnp.int32),
            pltpu.SMEM(cover.shape, jnp.int32),
            pltpu.SMEM(cover_count.shape, jnp.int32),
            pltpu.VMEM(blocks.shape, bf16),
            pltpu.VMEM(ocean_map.shape, jnp.int32),
            pltpu.VMEM((256, BS), bf16),
            pltpu.VMEM((ABLK, 256, NB * BS), bf16),
            pltpu.VMEM((16 * F, 2 * BS), bf16),
            pltpu.VMEM((32 * FP, BS), f32),
            pltpu.VMEM((32 * FP, BS), f32),
            pltpu.VMEM((F // 4, BS, BS), f32),
            pltpu.VMEM((32, BS), jnp.int32),
            pltpu.VMEM((ABLK, 2, 8, BS), bf16),
            pltpu.VMEM((ABLK, 2, 4, BS), bf16),
            pltpu.VMEM((OBLK * FP, BS), f32),
            pltpu.VMEM((Y * Z, 2 * BS), f32),
            pltpu.VMEM((2, BS, BS), f32),
            pltpu.VMEM((YL, F, BS), bf16),
            pltpu.VMEM((YL, F, BS), bf16),
            pltpu.VMEM((Z, F // 4, 4, BS), bf16),
            pltpu.VMEM((Z, F // 4, 4, BS), bf16),
            pltpu.VMEM((L, CAP, 2, 8, BS), bf16),
            pltpu.VMEM((L * CAP, 2, 8, BS), bf16),
            pltpu.VMEM((L, CAP, 2, 4, BS), bf16),
            pltpu.VMEM((L * CAP, 2, 4, BS), bf16),
            pltpu.VMEM((L, CAP, F // 4, 4, BS), bf16),
            pltpu.VMEM((L * CAP, F // 4, 4, BS), bf16),
            pltpu.VMEM((Z, 1, 2 * BS), f32),
            pltpu.VMEM((Y, Z, 1, 2 * BS), f32),
            pltpu.SemaphoreType.DMA((10,)),
            pltpu.SemaphoreType.DMA((7,)),
            pltpu.SemaphoreType.DMA((7,)),
            pltpu.SemaphoreType.REGULAR,
        ],
        compiler_params=pltpu.CompilerParams(
            collective_id=0, has_side_effects=True, vmem_limit_bytes=62 * 2**20
        ),
    )(
        atm_flux,
        cell_map,
        neighbours,
        coef_x,
        coef_y,
        jnp.swapaxes(send_list, 1, 2),
        cover,
        cover_count,
        blocks,
        ocean_map,
    )


def solution(mesh):
    return jax.shard_map(
        shards,
        mesh=mesh,
        in_specs=(
            P(None, ("region", "local")),
            P(("region", "local"), None),
            P(None, ("region", "local")),
            P(None, ("region", "local")),
            P(None, ("region", "local")),
            P(("region", "local"), None, None),
            P(("region", "local"), None),
            P(("region", "local")),
            P(("region", "local"), None, None, None, None),
            P(("region", "local"), None),
        ),
        out_specs=P(None, ("region", "local")),
        check_vma=False,
    )
```
